32 devices in a mesh: groups: 2 (over y), band: 4 (over z), comp: 2 (over x), sub: 2 (over core).
Axes of the slice: x: 2, y: 2, z: 4, core: 2. Of those that a mesh axis runs over, the one named last changes fastest.
Arguments:
- orbitals: float32 [1024, 16384], P(('groups', 'band'), ('comp', 'sub')), parts along dimension 0, may hold values from -6 to 6
- potential: float32 [32768], P(('groups', 'comp', 'sub')), parts along dimension 0, may hold values from 0.5 to 8
- proj_values: float32 [64, 4, 1024], P('groups'), parts along dimension 0, may hold values from -6 to 6
- block_list: int32 [64, 8], P('groups'), parts along dimension 0, may hold values from 0 to 127
- proj_energy: float32 [64, 4], P('groups'), parts along dimension 0, may hold values from 4 to 32
Outputs:
- updated: float32 [1024, 16384], P(('groups', 'band'), ('comp', 'sub')), parts along dimension 0
The draws below stay inside these ranges and needn't reach their ends.
There are 2 independent parts, one for each index of `groups`. The reference program is written for one: setup_inputs(seed, part) draws one part's arguments, and reference() takes and returns one part's arrays. A program takes and returns all parts, laid end to end along the dimension named above; each array names one. Nothing has to cross between parts.
Inputs may be any that keep to these rules, and one draw needn't show every extreme that they name: `block_list`: an atom's list may name a block more than once.
All inputs are finite; a program needn't handle non-finite values.
Results may differ from the reference program's by a relative error of at most 0.00014.
Values sent between devices are 32-bit elements; how exact they have to be, the bound alone decides.
A program may use at most 64 MiB of HBM per device.

```python
import math
import jax
import jax.numpy as jnp
from jax import lax

NORB = 512
NATOM = 32
NPA = 4
NBLK = 8
NC = 16384


def place_ends(values, own_key, low, high):
    index_at = [jax.random.randint(jax.random.fold_in(own_key, axis), (), 0, length) for axis, length in enumerate(values.shape)]
    widest = values.shape.index(max(values.shape))
    next_to = index_at[:widest] + [(index_at[widest] + 1) % values.shape[widest]] + index_at[widest + 1:]
    return values.at[tuple(index_at)].set(low).at[tuple(next_to)].set(high)


def raised(entries, key, source, target, blocks, factor):
    def block_of(axis_at):
        return (jnp.arange(entries.shape[axis_at]) // (entries.shape[axis_at] // blocks)).reshape((-1,) + (1,) * (entries.ndim - 1 - axis_at))

    near = jax.random.permutation(key, blocks)[block_of(target)]
    other_side = (block_of(target) + blocks // 2) % blocks
    return jnp.where((block_of(source) == near) | (block_of(source) == other_side), factor * entries, entries)


def levels(own_key, shape, shards, least, high):
    def one(dim, blocks):
        heights = jax.random.uniform(jax.random.fold_in(jax.random.fold_in(own_key, 6), dim), (blocks,), jnp.float32, least / len(shards), high / len(shards))
        return jnp.repeat(jnp.exp(heights), shape[dim] // blocks).reshape((-1,) + (1,) * (len(shape) - dim - 1))

    gain = one(*shards[0])
    for cut in shards[1:]:
        gain = gain * one(*cut)
    return gain


def centred(rng, shape, deviation, bound, pieces=(), kind=jnp.bfloat16):
    gain = levels(rng, shape, pieces, -0.22, 0.18) if pieces else 1.0
    array = jax.random.normal(rng, shape, jnp.float32) * deviation * gain
    return jnp.minimum(jnp.maximum(array, -bound), bound).astype(kind)


def bell_draw_with(own_key, dims, spread, limit, split, heavy, held_as=jnp.bfloat16):
    result = spread * jax.random.normal(own_key, dims, jnp.float32)
    if split:
        result = result * levels(own_key, dims, split, -0.22, 0.18)
    return jnp.clip(raised(result, jax.random.fold_in(own_key, 3), *heavy), -limit, limit).astype(held_as)


def setup_inputs(seed: int = 0, part: int = 0) -> dict:
    keys = jax.random.split(jax.random.key(seed), 6)
    part_splits = jax.random.split(jax.random.fold_in(keys[5], part), 6)
    return {
        "orbitals": bell_draw_with(part_splits[0], (NORB, NC), 1.0, 6.0, ((0, 4), (1, 4)), (1, 0, 4, 2.0), jnp.float32),
        "potential": jnp.clip(jnp.exp(math.log(8.0) - 2.7725887 * jax.random.uniform(part_splits[1], (NC,), jnp.float32) ** levels(part_splits[1], (NC,), ((0, 4),), -0.2, 0.2)), 0.5, 8.0),
        "proj_values": centred(part_splits[2], (NATOM, NPA, NBLK * 128), 1.0, 6.0, (), jnp.float32),
        "block_list": place_ends(jax.random.randint(part_splits[3], (NATOM, NBLK), 0, NC // 128), jax.random.fold_in(part_splits[3], 1), 0, (NC // 128) - 1).astype(jnp.int32),
        "proj_energy": jnp.clip(jnp.exp(jax.random.uniform(part_splits[4], (NATOM, NPA), jnp.float32, math.log(4.0), math.log(32.0))), 4.0, 32.0),
    }


step_size = 0.5

def reference(orbitals, potential, proj_values, block_list, proj_energy):
    highest = lax.Precision.HIGHEST
    proj_norm = 1.0 / math.sqrt(NBLK * 128)
    tiles = orbitals.reshape(NORB, NC // 128, 128)
    picked = tiles[:, block_list]
    proj_four = proj_values.reshape(NATOM, NPA, NBLK, 128)
    coupling = jnp.einsum('akbc,iabc->aki', proj_four, picked, precision=highest) * proj_norm
    weighted = proj_four * proj_energy[:, :, None, None]
    contrib = jnp.einsum('akbc,aki->iabc', weighted, coupling, precision=highest) * proj_norm
    extra = jnp.zeros_like(tiles).at[:, block_list].add(contrib)
    hpsi = potential[None, :] * orbitals + extra.reshape(NORB, NC)
    correlation = jnp.dot(orbitals, orbitals.T, precision=highest, preferred_element_type=jnp.float32) * (1.0 / NC)
    hmat = jnp.dot(orbitals, hpsi.T, precision=highest, preferred_element_type=jnp.float32) * (1.0 / NC)
    identity = jnp.eye(NORB, dtype=jnp.float32)
    lagrange = 0.5 * (hmat + hmat.T)
    orthogonal = 1.5 * identity - 0.5 * correlation
    mix_psi = jnp.dot(orthogonal, identity + step_size * lagrange, precision=highest, preferred_element_type=jnp.float32)
    mix_h = -step_size * orthogonal
    updated = jnp.dot(mix_psi, orbitals, precision=highest, preferred_element_type=jnp.float32)
    updated = updated + jnp.dot(mix_h, hpsi, precision=highest, preferred_element_type=jnp.float32)
    return updated
```

```python
import functools
import math

import jax
import jax.numpy as jnp
from jax import lax
from jax.experimental import pallas as pl
from jax.experimental.pallas import tpu as pltpu
from jax.sharding import PartitionSpec as P

step_size = 0.5
TILE = 128
CHUNK = 256
MESH = pl.DeviceIdType.MESH


def split(value):
    high = value.astype(jnp.bfloat16)
    low = (value - high.astype(jnp.float32)).astype(jnp.bfloat16)
    return high, low


def dot3(a, b, contract):
    dims = (((1,), (contract,)), ((), ()))
    one = functools.partial(
        lax.dot_general, dimension_numbers=dims, preferred_element_type=jnp.float32
    )
    return one(a[0], b[0]) + (one(a[0], b[1]) + one(a[1], b[0]))


def pair_index(i, j):
    return j * (j + 1) // 2 + i


def step_kernel(sizes, x_ref, v_ref, proj_ref, blk_ref, en_ref, out_ref,
                xs, y_hi, y_lo, red, fin, lm_hi, lm_lo, om_hi, om_lo, res,
                sub_box, comp_box, band_box, own_sem,
                in_send, in_recv, out_send, out_recv, keep_sem,
                rs_send, rs_recv, ag_send, ag_recv):
    nband, ncomp, nsub = sizes
    rows = x_ref.shape[0]
    norb, own = xs.shape
    nproj = proj_ref.shape[0]
    nblk = blk_ref.shape[1]
    chunks = own // CHUNK
    tri = norb // TILE
    pairs = tri * (tri + 1) // 2
    total_coef = own * nband * ncomp * nsub
    norm = 1.0 / math.sqrt(nblk * TILE)
    band = lax.axis_index("band")
    comp = lax.axis_index("comp")
    sub = lax.axis_index("sub")
    axes = {"band": (nband, band), "comp": (ncomp, comp), "sub": (nsub, sub)}

    barrier = pltpu.get_barrier_semaphore()
    for name, (count, me) in axes.items():
        for d in range(1, count):
            pl.semaphore_signal(barrier, inc=1, device_id={name: lax.rem(me + d, count)},
                                device_id_type=MESH)
    pl.semaphore_wait(barrier, nband + ncomp + nsub - 3)

    def cols_at(k):
        return pl.ds(pl.multiple_of(k * CHUNK, CHUNK), CHUNK)

    def wide_at(owner, k):
        return pl.ds(pl.multiple_of(owner * own + k * CHUNK, CHUNK), CHUNK)

    def rows_at(owner):
        return pl.ds(pl.multiple_of(owner * rows, rows), rows)

    def in_copy(k, d):
        peer = lax.rem(band + d, nband)
        return pltpu.make_async_remote_copy(
            src_ref=x_ref.at[:, wide_at(peer, k)],
            dst_ref=xs.at[rows_at(band), cols_at(k)],
            send_sem=in_send.at[k, d - 1], recv_sem=in_recv.at[k, d - 1],
            device_id={"band": peer}, device_id_type=MESH)

    @pl.loop(0, chunks)
    def _(k):
        for d in range(1, nband):
            in_copy(k, d).start()

    local = pltpu.make_async_copy(
        x_ref.at[:, pl.ds(pl.multiple_of(band * own, own), own)], xs.at[rows_at(band)], own_sem)
    local.start()

    red[...] = jnp.zeros_like(red)
    first_tile = ((comp * nsub + sub) * nband + band) * (own // TILE)

    @pl.loop(0, own // TILE)
    def _(t):
        dense = jnp.zeros((nproj, TILE), jnp.float32)
        for b in range(nblk):
            hit = blk_ref[:, b:b + 1] == first_tile + t
            dense = dense + jnp.where(hit, proj_ref[:, b * TILE:(b + 1) * TILE], 0.0)
        at = pl.ds(pl.multiple_of(t * TILE, TILE), TILE)
        high, low = split(dense)
        y_hi[norb:, at] = high
        y_lo[norb:, at] = low

    local.wait()

    @pl.loop(0, chunks)
    def _(k):
        for d in range(1, nband):
            in_copy(k, d).wait_recv()
        at = cols_at(k)
        x = xs[:, at]
        xd = split(x)
        y_hi[:norb, at] = xd[0]
        y_lo[:norb, at] = xd[1]
        wd = split(x * v_ref[:, wide_at(band, k)])
        for base, right in ((0, xd), (pairs, wd)):
            for j0 in range(0, tri, 2):
                j1 = min(j0 + 2, tri)
                left = (xd[0][:j1 * TILE], xd[1][:j1 * TILE])
                some = (right[0][j0 * TILE:j1 * TILE], right[1][j0 * TILE:j1 * TILE])
                part = dot3(left, some, 1)
                for j in range(j0, j1):
                    for i in range(j + 1):
                        here = (base + pair_index(i, j)) * TILE
                        red[here:here + TILE] += part[
                            i * TILE:(i + 1) * TILE, (j - j0) * TILE:(j - j0 + 1) * TILE]
        part = dot3(xd, (y_hi[norb:, at], y_lo[norb:, at]), 1)
        red[2 * pairs * TILE:2 * pairs * TILE + norb] += part

    def slab(start, size):
        return pl.ds(pl.multiple_of(start, 8), size)

    low, size = 0, red.shape[0]
    stages = []
    count_before = 0
    for name, box in (("sub", sub_box), ("comp", comp_box), ("band", band_box)):
        count, me = axes[name]
        piece = size // count
        copies = []
        for d in range(1, count):
            peer = lax.rem(me + d, count)
            at = count_before + d - 1
            copies.append(pltpu.make_async_remote_copy(
                src_ref=red.at[slab(low + peer * piece, piece)], dst_ref=box.at[d - 1],
                send_sem=rs_send.at[at], recv_sem=rs_recv.at[at],
                device_id={name: peer}, device_id_type=MESH))
        for copy in copies:
            copy.start()
        mine = low + me * piece
        for d, copy in enumerate(copies):
            copy.wait_recv()
            red[slab(mine, piece)] += box[d]
        for copy in copies:
            copy.wait_send()
        low, size = mine, piece
        stages.append((name, low, size, count_before))
        count_before += count - 1

    fin[slab(low, size)] = red[slab(low, size)]
    for name, start, length, before in reversed(stages):
        count, me = axes[name]
        copies = []
        for d in range(1, count):
            copies.append(pltpu.make_async_remote_copy(
                src_ref=fin.at[slab(start, length)], dst_ref=fin.at[slab(start, length)],
                send_sem=ag_send.at[before + d - 1], recv_sem=ag_recv.at[before + d - 1],
                device_id={name: lax.rem(me + d, count)}, device_id_type=MESH))
        for copy in copies:
            copy.start()
        for copy in copies:
            copy.wait()

    coupling = fin[2 * pairs * TILE:2 * pairs * TILE + norb] * norm
    strong = coupling * en_ref[...]
    strong_d = split(strong)
    coupling_d = split(coupling)
    last = split(strong * (-step_size * norm))
    lm_hi[:, norb:] = last[0]
    lm_lo[:, norb:] = last[1]
    for j in range(tri):
        js = slice(j * TILE, (j + 1) * TILE)
        nonlocal_part = dot3(
            (strong_d[0][:(j + 1) * TILE], strong_d[1][:(j + 1) * TILE]),
            (coupling_d[0][js], coupling_d[1][js]), 1)
        for i in range(j + 1):
            is_ = slice(i * TILE, (i + 1) * TILE)
            here = pair_index(i, j) * TILE
            corr = fin[here:here + TILE] * (-0.5 / total_coef)
            here = (pairs + pair_index(i, j)) * TILE
            lag = (fin[here:here + TILE] + nonlocal_part[is_]) * (step_size / total_coef)
            for value, hi_ref, lo_ref in ((corr, om_hi, om_lo), (lag, lm_hi, lm_lo)):
                hi, lo = split(value)
                hi_ref[is_, js] = hi
                lo_ref[is_, js] = lo
                if i != j:
                    hi, lo = split(value.T)
                    hi_ref[js, is_] = hi
                    lo_ref[js, is_] = lo

    def out_copy(k, d):
        peer = lax.rem(band + d, nband)
        return pltpu.make_async_remote_copy(
            src_ref=res.at[rows_at(peer), cols_at(k)],
            dst_ref=out_ref.at[:, wide_at(band, k)],
            send_sem=out_send.at[k, d - 1], recv_sem=out_recv.at[k, d - 1],
            device_id={"band": peer}, device_id_type=MESH)

    def keep_copy(k):
        return pltpu.make_async_copy(
            res.at[rows_at(band), cols_at(k)], out_ref.at[:, wide_at(band, k)], keep_sem.at[k])

    @pl.loop(0, chunks)
    def _(k):
        at = cols_at(k)
        x = xs[:, at]
        z = x - step_size * (x * v_ref[:, wide_at(band, k)])
        z = z + dot3((lm_hi[...], lm_lo[...]), (y_hi[:, at], y_lo[:, at]), 0)
        res[:, at] = 1.5 * z + dot3((om_hi[...], om_lo[...]), split(z), 0)
        for d in range(1, nband):
            out_copy(k, d).start()
        keep_copy(k).start()

    @pl.loop(0, chunks)
    def _(k):
        for d in range(1, nband):
            in_copy(k, d).wait_send()
            out_copy(k, d).wait()
        keep_copy(k).wait()


def on_device(orbitals, potential, proj_values, block_list, proj_energy):
    nband, ncomp, nsub = (lax.axis_size(name) for name in ("band", "comp", "sub"))
    atom_count, proj_count, proj_len = proj_values.shape
    nproj = atom_count * proj_count
    rows, row_width = orbitals.shape
    norb, own = rows * nband, row_width // nband
    chunks = own // CHUNK
    proj = proj_values.reshape(nproj, proj_len)
    blocks = jnp.repeat(block_list, proj_count, axis=0)
    energy = proj_energy.reshape(1, nproj)
    tri = norb // TILE
    need = tri * (tri + 1) * TILE + norb
    unit = 8 * nband * ncomp * nsub
    full = -(-need // unit) * unit
    f32, bf16, dma = jnp.float32, jnp.bfloat16, pltpu.SemaphoreType.DMA
    hops = nband + ncomp + nsub - 3
    half, quarter = full // nsub, full // (nsub * ncomp)
    vmem = pl.BlockSpec(memory_space=pltpu.VMEM)
    return pl.pallas_call(
        functools.partial(step_kernel, (nband, ncomp, nsub)),
        out_shape=jax.ShapeDtypeStruct(orbitals.shape, f32),
        in_specs=[pl.BlockSpec(memory_space=pl.ANY), vmem, vmem, vmem, vmem],
        out_specs=pl.BlockSpec(memory_space=pl.ANY),
        scratch_shapes=[
            pltpu.VMEM((norb, own), f32),
            pltpu.VMEM((norb + nproj, own), bf16),
            pltpu.VMEM((norb + nproj, own), bf16),
            pltpu.VMEM((full, TILE), f32),
            pltpu.VMEM((full, TILE), f32),
            pltpu.VMEM((norb, norb + nproj), bf16),
            pltpu.VMEM((norb, norb + nproj), bf16),
            pltpu.VMEM((norb, norb), bf16),
            pltpu.VMEM((norb, norb), bf16),
            pltpu.VMEM((norb, own), f32),
            pltpu.VMEM((nsub - 1, half, TILE), f32),
            pltpu.VMEM((ncomp - 1, quarter, TILE), f32),
            pltpu.VMEM((nband - 1, quarter // nband, TILE), f32),
            dma,
            dma((chunks, nband - 1)), dma((chunks, nband - 1)),
            dma((chunks, nband - 1)), dma((chunks, nband - 1)),
            dma((chunks,)),
            dma((hops,)), dma((hops,)), dma((hops,)), dma((hops,)),
        ],
        compiler_params=pltpu.CompilerParams(
            collective_id=0, has_side_effects=True, vmem_limit_bytes=48 * 1024 * 1024),
    )(orbitals, potential.reshape(1, row_width), proj, blocks, energy)


def solution(mesh):
    in_specs = (
        P(("groups", "band"), ("comp", "sub")),
        P(("groups", "comp", "sub")),
        P("groups", None, None),
        P("groups", None),
        P("groups", None),
    )
    out_specs = P(("groups", "band"), ("comp", "sub"))
    return jax.shard_map(
        on_device, mesh=mesh, in_specs=in_specs, out_specs=out_specs, check_vma=False
    )
```

```python
import functools
import math

import jax
import jax.numpy as jnp
from jax import lax
from jax.experimental import pallas as pl
from jax.experimental.pallas import tpu as pltpu
from jax.sharding import PartitionSpec as P

step_size = 0.5
TILE = 128
CHUNK = 256
MESH = pl.DeviceIdType.MESH


def split(value):
    high = value.astype(jnp.bfloat16)
    low = (value - high.astype(jnp.float32)).astype(jnp.bfloat16)
    return high, low


def dot3(a, b, contract):
    dims = (((1,), (contract,)), ((), ()))
    one = functools.partial(
        lax.dot_general, dimension_numbers=dims, preferred_element_type=jnp.float32
    )
    return one(a[0], b[0]) + (one(a[0], b[1]) + one(a[1], b[0]))


def pair_index(i, j, early):
    return j * (j - 1) // 2 + i if early else j * (j + 1) // 2 + i


def step_kernel(sizes, x_ref, v_ref, proj_ref, blk_ref, en_ref, out_ref,
                xs, y_hi, y_lo, red, fin, lm_hi, lm_lo, om_hi, om_lo, res,
                sub_box, comp_box, band_box, own_sem,
                in_send, in_recv, out_send, out_recv, keep_sem,
                sub_send, sub_recv, comp_send, comp_recv, band_send, band_recv,
                proj_buf, proj_sem, *more):
    nband, ncomp, nsub = sizes
    rows = x_ref.shape[0]
    norb, own = xs.shape
    nproj = proj_ref.shape[0]
    early = bool(more)
    nblk = blk_ref.shape[1]
    chunks = own // CHUNK
    tri = norb // TILE
    pairs = tri * (tri - 1) // 2 if early else tri * (tri + 1) // 2
    total_coef = own * nband * ncomp * nsub
    norm = 1.0 / math.sqrt(nblk * TILE)
    band = lax.axis_index("band")
    comp = lax.axis_index("comp")
    sub = lax.axis_index("sub")
    axes = {"band": (nband, band), "comp": (ncomp, comp), "sub": (nsub, sub)}

    barrier = pltpu.get_barrier_semaphore()
    for name, (count, me) in axes.items():
        for d in range(1, count):
            pl.semaphore_signal(barrier, inc=1, device_id={name: lax.rem(me + d, count)},
                                device_id_type=MESH)
    pl.semaphore_wait(barrier, nband + ncomp + nsub - 3)

    def cols_at(k):
        return pl.ds(pl.multiple_of(k * CHUNK, CHUNK), CHUNK)

    def wide_at(owner, k):
        return pl.ds(pl.multiple_of(owner * own + k * CHUNK, CHUNK), CHUNK)

    def rows_at(owner):
        return pl.ds(pl.multiple_of(owner * rows, rows), rows)

    def in_copy(k, d):
        peer = lax.rem(band + d, nband)
        return pltpu.make_async_remote_copy(
            src_ref=x_ref.at[:, wide_at(peer, k)],
            dst_ref=xs.at[rows_at(band), cols_at(k)],
            send_sem=in_send.at[k, d - 1], recv_sem=in_recv.at[k, d - 1],
            device_id={"band": peer}, device_id_type=MESH)

    @pl.loop(0, chunks)
    def _(k):
        for d in range(1, nband):
            in_copy(k, d).start()

    local = pltpu.make_async_copy(
        x_ref.at[:, pl.ds(pl.multiple_of(band * own, own), own)], xs.at[rows_at(band)], own_sem)
    local.start()
    get_proj = pltpu.make_async_copy(proj_ref, proj_buf, proj_sem)
    get_proj.start()
    if early:
        (x_own, p_hi, p_lo, part, sums, half_box, quarter_box, x_sem,
         e_send, e_recv, f_send, f_recv) = more
        get_x = pltpu.make_async_copy(x_ref, x_own, x_sem)
        get_x.start()
    red[...] = jnp.zeros_like(red)
    get_proj.wait()

    def dense_tile(tile):
        dense = jnp.zeros((nproj, TILE), jnp.float32)
        for b in range(nblk):
            hit = blk_ref[:, b:b + 1] == tile
            dense = dense + jnp.where(hit, proj_buf[:, b * TILE:(b + 1) * TILE], 0.0)
        return split(dense)

    here_first = (comp * nsub + sub) * nband * (own // TILE)
    if early:
        part[...] = jnp.zeros_like(part)
        get_x.wait()

        @pl.loop(0, nband * own // CHUNK)
        def _(k):
            tiles = [dense_tile(here_first + k * (CHUNK // TILE) + t)
                     for t in range(CHUNK // TILE)]
            p_d = tuple(jnp.concatenate([t[h] for t in tiles], axis=1) for h in range(2))
            at = cols_at(k)
            p_hi[:, at] = p_d[0]
            p_lo[:, at] = p_d[1]
            x = x_own[:, at]
            x_d = split(x)
            part[:TILE] += dot3(x_d, x_d, 1)
            part[TILE:2 * TILE] += dot3(x_d, split(x * v_ref[:, at]), 1)
            part[2 * TILE:] += dot3(x_d, p_d, 1)

        mine_cols = pl.ds(pl.multiple_of(band * own, own), own)
        y_hi[norb:] = p_hi[:, mine_cols]
        y_lo[norb:] = p_lo[:, mine_cols]
    else:
        @pl.loop(0, own // TILE)
        def _(t):
            at = pl.ds(pl.multiple_of(t * TILE, TILE), TILE)
            high, low = dense_tile(here_first + band * (own // TILE) + t)
            y_hi[norb:, at] = high
            y_lo[norb:, at] = low

    def slab(start, size):
        return pl.ds(pl.multiple_of(start, 8), size)

    def remote(src, dst, send, recv, name, d):
        count, me = axes[name]
        return pltpu.make_async_remote_copy(
            src_ref=src, dst_ref=dst, send_sem=send, recv_sem=recv,
            device_id={name: lax.rem(me + d, count)}, device_id_type=MESH)

    if early:
        e_low, e_size, before = 0, 3 * TILE, 0
        for name, box in (("sub", half_box), ("comp", quarter_box)):
            count, me = axes[name]
            e_size //= count
            copies = [
                remote(part.at[slab(e_low + lax.rem(me + d, count) * e_size, e_size)],
                       box.at[d - 1], e_send.at[before + d - 1], e_recv.at[before + d - 1],
                       name, d)
                for d in range(1, count)]
            for copy in copies:
                copy.start()
            e_low = e_low + me * e_size
            for d, copy in enumerate(copies):
                copy.wait_recv()
                part[slab(e_low, e_size)] += box[d]
            for copy in copies:
                copy.wait_send()
            before += count - 1
        sums[band, slab(e_low, e_size)] = part[slab(e_low, e_size)]
        mine = sums.at[band, slab(e_low, e_size)]
        e_band = [remote(mine, mine, f_send.at[d - 1], f_recv.at[d - 1], "band", d)
                  for d in range(1, nband)]
        for copy in e_band:
            copy.start()

    local.wait()

    @pl.loop(0, chunks)
    def _(k):
        for d in range(1, nband):
            in_copy(k, d).wait_recv()
        at = cols_at(k)
        x = xs[:, at]
        xd = split(x)
        y_hi[:norb, at] = xd[0]
        y_lo[:norb, at] = xd[1]
        wd = split(x * v_ref[:, wide_at(band, k)])
        for base, right in ((0, xd), (pairs, wd)):
            for j0 in range(0, tri, 2):
                j1 = min(j0 + 2, tri)
                j0 = max(j0, 1) if early else j0
                reach = (j1 - 1 if early else j1) * TILE
                left = (xd[0][:reach], xd[1][:reach])
                some = (right[0][j0 * TILE:j1 * TILE], right[1][j0 * TILE:j1 * TILE])
                got = dot3(left, some, 1)
                for j in range(j0, j1):
                    for i in range(j if early else j + 1):
                        here = (base + pair_index(i, j, early)) * TILE
                        red[here:here + TILE] += got[
                            i * TILE:(i + 1) * TILE, (j - j0) * TILE:(j - j0 + 1) * TILE]
        if not early:
            red[2 * pairs * TILE:2 * pairs * TILE + norb] += dot3(
                xd, (y_hi[norb:, at], y_lo[norb:, at]), 1)

    half = red.shape[0] // nsub
    quarter = half // ncomp
    unit = quarter // nband
    half_low = sub * half
    low = half_low + comp * quarter
    own_low = low + band * unit

    to_sub = [remote(red.at[slab(lax.rem(sub + d, nsub) * half, half)], sub_box.at[d - 1],
                     sub_send.at[0, d - 1], sub_recv.at[0, d - 1], "sub", d)
              for d in range(1, nsub)]
    for copy in to_sub:
        copy.start()
    for d, copy in enumerate(to_sub):
        copy.wait_recv()
        red[slab(half_low, half)] += sub_box[d]

    to_comp = [[remote(red.at[slab(half_low + lax.rem(comp + d, ncomp) * quarter
                                   + lax.rem(band + q, nband) * unit, unit)],
                       comp_box.at[d - 1, lax.rem(band + q, nband)],
                       comp_send.at[0, d - 1, lax.rem(band + q, nband)],
                       comp_recv.at[0, d - 1, lax.rem(band + q, nband)], "comp", d)
                for d in range(1, ncomp)] for q in range(1, nband + 1)]
    for copies in to_comp:
        for copy in copies:
            copy.start()
    to_band = []
    for q in range(1, nband + 1):
        owner = lax.rem(band + q, nband)
        piece = slab(low + owner * unit, unit)
        for d, copy in enumerate(to_comp[q - 1]):
            copy.wait_recv()
            red[piece] += comp_box[d, owner]
        if q < nband:
            copy = remote(red.at[piece], band_box.at[q - 1],
                          band_send.at[0, q - 1], band_recv.at[0, q - 1], "band", q)
            copy.start()
            to_band.append(copy)
    if early:
        for copy in e_band:
            copy.wait_recv()
        every = sums.at[:, slab(e_low, e_size)]
        e_comp = [remote(every, every, e_send.at[before + d - 1], e_recv.at[before + d - 1],
                         "comp", d) for d in range(1, ncomp)]
        for copy in e_comp:
            copy.start()
    for d, copy in enumerate(to_band):
        copy.wait_recv()
        red[slab(own_low, unit)] += band_box[d]

    fin[slab(own_low, unit)] = red[slab(own_low, unit)]
    mine = fin.at[slab(own_low, unit)]
    back_band = [remote(mine, mine, band_send.at[1, d - 1], band_recv.at[1, d - 1], "band", d)
                 for d in range(1, nband)]
    for copy in back_band:
        copy.start()
    back_comp = []
    for q in range(nband):
        if q:
            back_band[q - 1].wait_recv()
        owner = lax.rem(band + nband - q, nband)
        piece = fin.at[slab(low + owner * unit, unit)]
        for d in range(1, ncomp):
            copy = remote(piece, piece, comp_send.at[1, d - 1, q], comp_recv.at[1, d - 1, q],
                          "comp", d)
            copy.start()
            back_comp.append(copy)
    if early:
        for copy in e_comp:
            copy.wait_recv()
        e_half = e_low - comp * e_size
        every = sums.at[:, slab(e_half, ncomp * e_size)]
        e_sub = [remote(every, every, e_send.at[before + ncomp - 1 + d - 1],
                        e_recv.at[before + ncomp - 1 + d - 1], "sub", d)
                 for d in range(1, nsub)]
        for copy in e_sub:
            copy.start()
    for copy in back_comp:
        copy.wait_recv()
    mine = fin.at[slab(half_low, half)]
    back_sub = [remote(mine, mine, sub_send.at[1, d - 1], sub_recv.at[1, d - 1], "sub", d)
                for d in range(1, nsub)]
    for copy in back_sub:
        copy.start()
    if early:
        for copy in e_sub:
            copy.wait_recv()
    for copy in back_sub:
        copy.wait_recv()

    def summed(kind, i, j):
        if early and i == j:
            return sums[i, kind * TILE:(kind + 1) * TILE]
        here = (kind * pairs + pair_index(i, j, early)) * TILE
        return fin[here:here + TILE]

    if early:
        coupling = jnp.concatenate([sums[i, 2 * TILE:] for i in range(tri)], axis=0) * norm
    else:
        coupling = fin[2 * pairs * TILE:2 * pairs * TILE + norb] * norm
    strong = coupling * en_ref[...]
    strong_d = split(strong)
    coupling_d = split(coupling)
    last = split(strong * (-step_size * norm))
    lm_hi[:, norb:] = last[0]
    lm_lo[:, norb:] = last[1]
    for j in range(tri):
        js = slice(j * TILE, (j + 1) * TILE)
        nonlocal_part = dot3(
            (strong_d[0][:(j + 1) * TILE], strong_d[1][:(j + 1) * TILE]),
            (coupling_d[0][js], coupling_d[1][js]), 1)
        for i in range(j + 1):
            is_ = slice(i * TILE, (i + 1) * TILE)
            corr = summed(0, i, j) * (-0.5 / total_coef)
            lag = (summed(1, i, j) + nonlocal_part[is_]) * (step_size / total_coef)
            for value, hi_ref, lo_ref in ((corr, om_hi, om_lo), (lag, lm_hi, lm_lo)):
                hi, lo = split(value)
                hi_ref[is_, js] = hi
                lo_ref[is_, js] = lo
                if i != j:
                    hi, lo = split(value.T)
                    hi_ref[js, is_] = hi
                    lo_ref[js, is_] = lo

    def out_copy(k, d):
        peer = lax.rem(band + d, nband)
        return pltpu.make_async_remote_copy(
            src_ref=res.at[rows_at(peer), cols_at(k)],
            dst_ref=out_ref.at[:, wide_at(band, k)],
            send_sem=out_send.at[k, d - 1], recv_sem=out_recv.at[k, d - 1],
            device_id={"band": peer}, device_id_type=MESH)

    def keep_copy(k):
        return pltpu.make_async_copy(
            res.at[rows_at(band), cols_at(k)], out_ref.at[:, wide_at(band, k)], keep_sem.at[k])

    @pl.loop(0, chunks)
    def _(k):
        at = cols_at(k)
        x = xs[:, at]
        z = x - step_size * (x * v_ref[:, wide_at(band, k)])
        z = z + dot3((lm_hi[...], lm_lo[...]), (y_hi[:, at], y_lo[:, at]), 0)
        res[:, at] = 1.5 * z + dot3((om_hi[...], om_lo[...]), split(z), 0)
        for d in range(1, nband):
            out_copy(k, d).start()
        keep_copy(k).start()

    @pl.loop(0, chunks)
    def _(k):
        for d in range(1, nband):
            in_copy(k, d).wait_send()
            out_copy(k, d).wait()
        keep_copy(k).wait()

    sent = to_sub + to_band + back_band + back_comp + back_sub
    for copies in to_comp:
        sent = sent + copies
    if early:
        sent = sent + e_band + e_comp + e_sub
    for copy in sent:
        copy.wait_send()


def on_device(orbitals, potential, proj_values, block_list, proj_energy):
    nband, ncomp, nsub = (lax.axis_size(name) for name in ("band", "comp", "sub"))
    atom_count, proj_count, proj_len = proj_values.shape
    nproj = atom_count * proj_count
    rows, row_width = orbitals.shape
    norb, own = rows * nband, row_width // nband
    chunks = own // CHUNK
    proj = proj_values.reshape(nproj, proj_len)
    blocks = jnp.repeat(block_list, proj_count, axis=0)
    energy = proj_energy.reshape(1, nproj)
    tri = norb // TILE
    early = rows == TILE and nproj == TILE and 3 * TILE % (8 * ncomp * nsub) == 0
    need = tri * (tri - 1) * TILE if early else tri * (tri + 1) * TILE + norb
    unit = 8 * nband * ncomp * nsub
    full = -(-need // unit) * unit
    f32, bf16, dma = jnp.float32, jnp.bfloat16, pltpu.SemaphoreType.DMA
    more = []
    if early:
        hops = 2 * (nsub + ncomp - 2)
        e_half = 3 * TILE // nsub
        more = [
            pltpu.VMEM((rows, row_width), f32),
            pltpu.VMEM((nproj, row_width), bf16),
            pltpu.VMEM((nproj, row_width), bf16),
            pltpu.VMEM((3 * TILE, TILE), f32),
            pltpu.VMEM((nband, 3 * TILE, TILE), f32),
            pltpu.VMEM((nsub - 1, e_half, TILE), f32),
            pltpu.VMEM((ncomp - 1, e_half // ncomp, TILE), f32),
            dma,
            dma((hops,)), dma((hops,)), dma((nband - 1,)), dma((nband - 1,)),
        ]
    half, quarter = full // nsub, full // (nsub * ncomp)
    anywhere = pl.BlockSpec(memory_space=pl.ANY)
    vmem = pl.BlockSpec(memory_space=pltpu.VMEM)
    return pl.pallas_call(
        functools.partial(step_kernel, (nband, ncomp, nsub)),
        out_shape=jax.ShapeDtypeStruct(orbitals.shape, f32),
        in_specs=[anywhere, vmem, anywhere, vmem, vmem],
        out_specs=anywhere,
        scratch_shapes=[
            pltpu.VMEM((norb, own), f32),
            pltpu.VMEM((norb + nproj, own), bf16),
            pltpu.VMEM((norb + nproj, own), bf16),
            pltpu.VMEM((full, TILE), f32),
            pltpu.VMEM((full, TILE), f32),
            pltpu.VMEM((norb, norb + nproj), bf16),
            pltpu.VMEM((norb, norb + nproj), bf16),
            pltpu.VMEM((norb, norb), bf16),
            pltpu.VMEM((norb, norb), bf16),
            pltpu.VMEM((norb, own), f32),
            pltpu.VMEM((nsub - 1, half, TILE), f32),
            pltpu.VMEM((ncomp - 1, nband, quarter // nband, TILE), f32),
            pltpu.VMEM((nband - 1, quarter // nband, TILE), f32),
            dma,
            dma((chunks, nband - 1)), dma((chunks, nband - 1)),
            dma((chunks, nband - 1)), dma((chunks, nband - 1)),
            dma((chunks,)),
            dma((2, nsub - 1)), dma((2, nsub - 1)),
            dma((2, ncomp - 1, nband)), dma((2, ncomp - 1, nband)),
            dma((2, nband - 1)), dma((2, nband - 1)),
            pltpu.VMEM((nproj, proj_len), f32), dma,
            *more,
        ],
        compiler_params=pltpu.CompilerParams(
            collective_id=0, has_side_effects=True, vmem_limit_bytes=48 * 1024 * 1024),
    )(orbitals, potential.reshape(1, row_width), proj, blocks, energy)


def solution(mesh):
    in_specs = (
        P(("groups", "band"), ("comp", "sub")),
        P(("groups", "comp", "sub")),
        P("groups", None, None),
        P("groups", None),
        P("groups", None),
    )
    out_specs = P(("groups", "band"), ("comp", "sub"))
    return jax.shard_map(
        on_device, mesh=mesh, in_specs=in_specs, out_specs=out_specs, check_vma=False
    )
```

```python
import functools
import math

import jax
import jax.numpy as jnp
from jax import lax
from jax.experimental import pallas as pl
from jax.experimental.pallas import tpu as pltpu
from jax.sharding import PartitionSpec as P

step_size = 0.5
TILE = 128
CHUNK = 256
MESH = pl.DeviceIdType.MESH


def split(value):
    high = value.astype(jnp.bfloat16)
    low = (value - high.astype(jnp.float32)).astype(jnp.bfloat16)
    return high, low


def dot3(a, b, contract):
    dims = (((1,), (contract,)), ((), ()))
    one = functools.partial(
        lax.dot_general, dimension_numbers=dims, preferred_element_type=jnp.float32
    )
    return one(a[0], b[0]) + (one(a[0], b[1]) + one(a[1], b[0]))


def pair_index(i, j, early):
    return j * (j - 1) // 2 + i if early else j * (j + 1) // 2 + i


def step_kernel(sizes, x_ref, v_ref, proj_ref, blk_ref, en_ref, out_ref,
                xs, y_hi, y_lo, red, fin, lm_hi, lm_lo, om_hi, om_lo, res,
                sub_box, comp_box, band_box, own_sem,
                in_send, in_recv, out_send, out_recv, keep_sem,
                sub_send, sub_recv, comp_send, comp_recv, band_send, band_recv,
                proj_buf, proj_sem, *more):
    nband, ncomp, nsub = sizes
    rows = x_ref.shape[0]
    norb, own = xs.shape
    nproj = proj_ref.shape[0]
    early = bool(more)
    nblk = blk_ref.shape[1]
    chunks = own // CHUNK
    tri = norb // TILE
    pairs = tri * (tri - 1) // 2 if early else tri * (tri + 1) // 2
    total_coef = own * nband * ncomp * nsub
    norm = 1.0 / math.sqrt(nblk * TILE)
    band = lax.axis_index("band")
    comp = lax.axis_index("comp")
    sub = lax.axis_index("sub")
    axes = {"band": (nband, band), "comp": (ncomp, comp), "sub": (nsub, sub)}

    barrier = pltpu.get_barrier_semaphore()
    for name, (count, me) in axes.items():
        for d in range(1, count):
            pl.semaphore_signal(barrier, inc=1, device_id={name: lax.rem(me + d, count)},
                                device_id_type=MESH)
    pl.semaphore_wait(barrier, nband + ncomp + nsub - 3)

    def cols_at(k):
        return pl.ds(pl.multiple_of(k * CHUNK, CHUNK), CHUNK)

    def wide_at(owner, k):
        return pl.ds(pl.multiple_of(owner * own + k * CHUNK, CHUNK), CHUNK)

    def rows_at(owner):
        return pl.ds(pl.multiple_of(owner * rows, rows), rows)

    def in_copy(k, d):
        peer = lax.rem(band + d, nband)
        return pltpu.make_async_remote_copy(
            src_ref=x_ref.at[:, wide_at(peer, k)],
            dst_ref=xs.at[rows_at(band), cols_at(k)],
            send_sem=in_send.at[k, d - 1], recv_sem=in_recv.at[k, d - 1],
            device_id={"band": peer}, device_id_type=MESH)

    @pl.loop(0, chunks)
    def _(k):
        for d in range(1, nband):
            in_copy(k, d).start()

    local = pltpu.make_async_copy(
        x_ref.at[:, pl.ds(pl.multiple_of(band * own, own), own)], xs.at[rows_at(band)], own_sem)
    local.start()
    get_proj = pltpu.make_async_copy(proj_ref, proj_buf, proj_sem)
    get_proj.start()
    if early:
        (x_own, p_hi, p_lo, part, sums, half_box, quarter_box, x_sem,
         e_send, e_recv, f_send, f_recv,
         xe, ze, rese, xe_send, xe_recv, side_send, side_recv, side_sem) = more
        get_x = pltpu.make_async_copy(x_ref, x_own, x_sem)
        get_x.start()
    red[...] = jnp.zeros_like(red)
    get_proj.wait()

    def dense_tile(tile):
        dense = jnp.zeros((nproj, TILE), jnp.float32)
        for b in range(nblk):
            hit = blk_ref[:, b:b + 1] == tile
            dense = dense + jnp.where(hit, proj_buf[:, b * TILE:(b + 1) * TILE], 0.0)
        return split(dense)

    here_first = (comp * nsub + sub) * nband * (own // TILE)
    if early:
        part[...] = jnp.zeros_like(part)
        get_x.wait()
        group = nband // 2
        first = band // group * group
        far = lax.rem(band + group, nband)
        xe[rows_at(band)] = x_own[:, wide_at(far, chunks - 1)]
        xe_copies = []
        for d in range(1, nband):
            to = lax.rem(band + d, nband)
            xe_copies.append(pltpu.make_async_remote_copy(
                src_ref=x_ref.at[:, wide_at(lax.rem(to + group, nband), chunks - 1)],
                dst_ref=xe.at[rows_at(band)],
                send_sem=xe_send.at[d - 1], recv_sem=xe_recv.at[d - 1],
                device_id={"band": to}, device_id_type=MESH))
        for copy in xe_copies:
            copy.start()

        @pl.loop(0, nband * own // CHUNK)
        def _(k):
            tiles = [dense_tile(here_first + k * (CHUNK // TILE) + t)
                     for t in range(CHUNK // TILE)]
            p_d = tuple(jnp.concatenate([t[h] for t in tiles], axis=1) for h in range(2))
            at = cols_at(k)
            p_hi[:, at] = p_d[0]
            p_lo[:, at] = p_d[1]
            x = x_own[:, at]
            x_d = split(x)
            part[:TILE] += dot3(x_d, x_d, 1)
            part[TILE:2 * TILE] += dot3(x_d, split(x * v_ref[:, at]), 1)
            part[2 * TILE:] += dot3(x_d, p_d, 1)

        mine_cols = pl.ds(pl.multiple_of(band * own, own), own)
        y_hi[norb:] = p_hi[:, mine_cols]
        y_lo[norb:] = p_lo[:, mine_cols]
    else:
        @pl.loop(0, own // TILE)
        def _(t):
            at = pl.ds(pl.multiple_of(t * TILE, TILE), TILE)
            high, low = dense_tile(here_first + band * (own // TILE) + t)
            y_hi[norb:, at] = high
            y_lo[norb:, at] = low

    def slab(start, size):
        return pl.ds(pl.multiple_of(start, 8), size)

    def remote(src, dst, send, recv, name, d):
        count, me = axes[name]
        return pltpu.make_async_remote_copy(
            src_ref=src, dst_ref=dst, send_sem=send, recv_sem=recv,
            device_id={name: lax.rem(me + d, count)}, device_id_type=MESH)

    if early:
        e_low, e_size, before = 0, 3 * TILE, 0
        for name, box in (("sub", half_box), ("comp", quarter_box)):
            count, me = axes[name]
            e_size //= count
            copies = [
                remote(part.at[slab(e_low + lax.rem(me + d, count) * e_size, e_size)],
                       box.at[d - 1], e_send.at[before + d - 1], e_recv.at[before + d - 1],
                       name, d)
                for d in range(1, count)]
            for copy in copies:
                copy.start()
            e_low = e_low + me * e_size
            for d, copy in enumerate(copies):
                copy.wait_recv()
                part[slab(e_low, e_size)] += box[d]
            for copy in copies:
                copy.wait_send()
            before += count - 1
        sums[band, slab(e_low, e_size)] = part[slab(e_low, e_size)]
        mine = sums.at[band, slab(e_low, e_size)]
        e_band = [remote(mine, mine, f_send.at[d - 1], f_recv.at[d - 1], "band", d)
                  for d in range(1, nband)]
        for copy in e_band:
            copy.start()

    local.wait()

    @pl.loop(0, chunks)
    def _(k):
        for d in range(1, nband):
            in_copy(k, d).wait_recv()
        at = cols_at(k)
        x = xs[:, at]
        xd = split(x)
        y_hi[:norb, at] = xd[0]
        y_lo[:norb, at] = xd[1]
        wd = split(x * v_ref[:, wide_at(band, k)])
        for base, right in ((0, xd), (pairs, wd)):
            for j0 in range(0, tri, 2):
                j1 = min(j0 + 2, tri)
                j0 = max(j0, 1) if early else j0
                reach = (j1 - 1 if early else j1) * TILE
                left = (xd[0][:reach], xd[1][:reach])
                some = (right[0][j0 * TILE:j1 * TILE], right[1][j0 * TILE:j1 * TILE])
                got = dot3(left, some, 1)
                for j in range(j0, j1):
                    for i in range(j if early else j + 1):
                        here = (base + pair_index(i, j, early)) * TILE
                        red[here:here + TILE] += got[
                            i * TILE:(i + 1) * TILE, (j - j0) * TILE:(j - j0 + 1) * TILE]
        if not early:
            red[2 * pairs * TILE:2 * pairs * TILE + norb] += dot3(
                xd, (y_hi[norb:, at], y_lo[norb:, at]), 1)

    half = red.shape[0] // nsub
    quarter = half // ncomp
    unit = quarter // nband
    half_low = sub * half
    low = half_low + comp * quarter
    own_low = low + band * unit

    to_sub = [remote(red.at[slab(lax.rem(sub + d, nsub) * half, half)], sub_box.at[d - 1],
                     sub_send.at[0, d - 1], sub_recv.at[0, d - 1], "sub", d)
              for d in range(1, nsub)]
    for copy in to_sub:
        copy.start()
    for d, copy in enumerate(to_sub):
        copy.wait_recv()
        red[slab(half_low, half)] += sub_box[d]

    to_comp = [[remote(red.at[slab(half_low + lax.rem(comp + d, ncomp) * quarter
                                   + lax.rem(band + q, nband) * unit, unit)],
                       comp_box.at[d - 1, lax.rem(band + q, nband)],
                       comp_send.at[0, d - 1, lax.rem(band + q, nband)],
                       comp_recv.at[0, d - 1, lax.rem(band + q, nband)], "comp", d)
                for d in range(1, ncomp)] for q in range(1, nband + 1)]
    for copies in to_comp:
        for copy in copies:
            copy.start()
    to_band = []
    for q in range(1, nband + 1):
        owner = lax.rem(band + q, nband)
        piece = slab(low + owner * unit, unit)
        for d, copy in enumerate(to_comp[q - 1]):
            copy.wait_recv()
            red[piece] += comp_box[d, owner]
        if q < nband:
            copy = remote(red.at[piece], band_box.at[q - 1],
                          band_send.at[0, q - 1], band_recv.at[0, q - 1], "band", q)
            copy.start()
            to_band.append(copy)
    if early:
        for copy in e_band:
            copy.wait_recv()
        every = sums.at[:, slab(e_low, e_size)]
        e_comp = [remote(every, every, e_send.at[before + d - 1], e_recv.at[before + d - 1],
                         "comp", d) for d in range(1, ncomp)]
        for copy in e_comp:
            copy.start()
    for d, copy in enumerate(to_band):
        copy.wait_recv()
        red[slab(own_low, unit)] += band_box[d]

    fin[slab(own_low, unit)] = red[slab(own_low, unit)]
    mine = fin.at[slab(own_low, unit)]
    back_band = [remote(mine, mine, band_send.at[1, d - 1], band_recv.at[1, d - 1], "band", d)
                 for d in range(1, nband)]
    for copy in back_band:
        copy.start()
    back_comp = []
    for q in range(nband):
        if q:
            back_band[q - 1].wait_recv()
        owner = lax.rem(band + nband - q, nband)
        piece = fin.at[slab(low + owner * unit, unit)]
        for d in range(1, ncomp):
            copy = remote(piece, piece, comp_send.at[1, d - 1, q], comp_recv.at[1, d - 1, q],
                          "comp", d)
            copy.start()
            back_comp.append(copy)
    if early:
        for copy in e_comp:
            copy.wait_recv()
        e_half = e_low - comp * e_size
        every = sums.at[:, slab(e_half, ncomp * e_size)]
        e_sub = [remote(every, every, e_send.at[before + ncomp - 1 + d - 1],
                        e_recv.at[before + ncomp - 1 + d - 1], "sub", d)
                 for d in range(1, nsub)]
        for copy in e_sub:
            copy.start()
    for copy in back_comp:
        copy.wait_recv()
    mine = fin.at[slab(half_low, half)]
    back_sub = [remote(mine, mine, sub_send.at[1, d - 1], sub_recv.at[1, d - 1], "sub", d)
                for d in range(1, nsub)]
    for copy in back_sub:
        copy.start()
    if early:
        for copy in e_sub:
            copy.wait_recv()
    for copy in back_sub:
        copy.wait_recv()

    def summed(kind, i, j):
        if early and i == j:
            return sums[i, kind * TILE:(kind + 1) * TILE]
        here = (kind * pairs + pair_index(i, j, early)) * TILE
        return fin[here:here + TILE]

    if early:
        coupling = jnp.concatenate([sums[i, 2 * TILE:] for i in range(tri)], axis=0) * norm
    else:
        coupling = fin[2 * pairs * TILE:2 * pairs * TILE + norb] * norm
    strong = coupling * en_ref[...]
    strong_d = split(strong)
    coupling_d = split(coupling)
    last = split(strong * (-step_size * norm))
    lm_hi[:, norb:] = last[0]
    lm_lo[:, norb:] = last[1]
    for j in range(tri):
        js = slice(j * TILE, (j + 1) * TILE)
        nonlocal_part = dot3(
            (strong_d[0][:(j + 1) * TILE], strong_d[1][:(j + 1) * TILE]),
            (coupling_d[0][js], coupling_d[1][js]), 1)
        for i in range(j + 1):
            is_ = slice(i * TILE, (i + 1) * TILE)
            corr = summed(0, i, j) * (-0.5 / total_coef)
            lag = (summed(1, i, j) + nonlocal_part[is_]) * (step_size / total_coef)
            for value, hi_ref, lo_ref in ((corr, om_hi, om_lo), (lag, lm_hi, lm_lo)):
                hi, lo = split(value)
                hi_ref[is_, js] = hi
                lo_ref[is_, js] = lo
                if i != j:
                    hi, lo = split(value.T)
                    hi_ref[js, is_] = hi
                    lo_ref[js, is_] = lo

    def out_copy(k, d):
        peer = lax.rem(band + d, nband)
        return pltpu.make_async_remote_copy(
            src_ref=res.at[rows_at(peer), cols_at(k)],
            dst_ref=out_ref.at[:, wide_at(band, k)],
            send_sem=out_send.at[k, d - 1], recv_sem=out_recv.at[k, d - 1],
            device_id={"band": peer}, device_id_type=MESH)

    def keep_copy(k):
        return pltpu.make_async_copy(
            res.at[rows_at(band), cols_at(k)], out_ref.at[:, wide_at(band, k)], keep_sem.at[k])

    def mixed(k):
        at = cols_at(k)
        x = xs[:, at]
        z = x - step_size * (x * v_ref[:, wide_at(band, k)])
        z = z + dot3((lm_hi[...], lm_lo[...]), (y_hi[:, at], y_lo[:, at]), 0)
        res[:, at] = 1.5 * z + dot3((om_hi[...], om_lo[...]), split(z), 0)
        keep_copy(k).start()

    over = chunks - 1 if early else chunks

    @pl.loop(0, over)
    def _(k):
        mixed(k)
        for d in range(1, nband):
            out_copy(k, d).start()

    if early:
        def side_copy(slot, d, src, owner):
            peer = lax.rem(band - first + d, group)
            return pltpu.make_async_remote_copy(
                src_ref=src(peer), dst_ref=out_ref.at[:, wide_at(owner, over)],
                send_sem=side_send.at[slot, d - 1], recv_sem=side_recv.at[slot, d - 1],
                device_id={"band": first + peer}, device_id_type=MESH)

        mixed(over)
        near_copies = [
            side_copy(0, d, lambda peer: res.at[rows_at(first + peer), cols_at(over)], band)
            for d in range(1, group)]
        for copy in near_copies:
            copy.start()
        for copy in xe_copies:
            copy.wait_recv()
        x = xe[...]
        x_d = split(x)
        far_cols = wide_at(far, over)
        z = x - step_size * (x * v_ref[:, far_cols])
        both = (jnp.concatenate([x_d[0], p_hi[:, far_cols]], axis=0),
                jnp.concatenate([x_d[1], p_lo[:, far_cols]], axis=0))
        z = z + dot3((lm_hi[...], lm_lo[...]), both, 0)
        ze[...] = z
        some = pl.ds(pl.multiple_of(first * rows, rows), group * rows)
        rese[...] = 1.5 * ze[some] + dot3((om_hi[some], om_lo[some]), split(z), 0)
        far_copies = [side_copy(1, d, lambda peer: rese.at[rows_at(peer)], far)
                      for d in range(1, group)]
        for copy in far_copies:
            copy.start()
        keep_far = pltpu.make_async_copy(
            rese.at[rows_at(band - first)], out_ref.at[:, far_cols], side_sem)
        keep_far.start()

    @pl.loop(0, chunks)
    def _(k):
        for d in range(1, nband):
            in_copy(k, d).wait_send()
        keep_copy(k).wait()

    @pl.loop(0, over)
    def _(k):
        for d in range(1, nband):
            out_copy(k, d).wait()

    if early:
        keep_far.wait()
        for copy in near_copies + far_copies:
            copy.wait()

    sent = to_sub + to_band + back_band + back_comp + back_sub
    for copies in to_comp:
        sent = sent + copies
    if early:
        sent = sent + e_band + e_comp + e_sub + xe_copies
    for copy in sent:
        copy.wait_send()


def on_device(orbitals, potential, proj_values, block_list, proj_energy):
    nband, ncomp, nsub = (lax.axis_size(name) for name in ("band", "comp", "sub"))
    atom_count, proj_count, proj_len = proj_values.shape
    nproj = atom_count * proj_count
    rows, row_width = orbitals.shape
    norb, own = rows * nband, row_width // nband
    chunks = own // CHUNK
    proj = proj_values.reshape(nproj, proj_len)
    blocks = jnp.repeat(block_list, proj_count, axis=0)
    energy = proj_energy.reshape(1, nproj)
    tri = norb // TILE
    early = rows == TILE and nband % 2 == 0 and nband > 2 and nproj == TILE and 3 * TILE % (8 * ncomp * nsub) == 0
    need = tri * (tri - 1) * TILE if early else tri * (tri + 1) * TILE + norb
    unit = 8 * nband * ncomp * nsub
    full = -(-need // unit) * unit
    f32, bf16, dma = jnp.float32, jnp.bfloat16, pltpu.SemaphoreType.DMA
    more = []
    if early:
        hops = 2 * (nsub + ncomp - 2)
        e_half = 3 * TILE // nsub
        more = [
            pltpu.VMEM((rows, row_width), f32),
            pltpu.VMEM((nproj, row_width), bf16),
            pltpu.VMEM((nproj, row_width), bf16),
            pltpu.VMEM((3 * TILE, TILE), f32),
            pltpu.VMEM((nband, 3 * TILE, TILE), f32),
            pltpu.VMEM((nsub - 1, e_half, TILE), f32),
            pltpu.VMEM((ncomp - 1, e_half // ncomp, TILE), f32),
            dma,
            dma((hops,)), dma((hops,)), dma((nband - 1,)), dma((nband - 1,)),
            pltpu.VMEM((norb, CHUNK), f32),
            pltpu.VMEM((norb, CHUNK), f32),
            pltpu.VMEM((norb // 2, CHUNK), f32),
            dma((nband - 1,)), dma((nband - 1,)),
            dma((2, nband // 2 - 1)), dma((2, nband // 2 - 1)), dma,
        ]
    half, quarter = full // nsub, full // (nsub * ncomp)
    anywhere = pl.BlockSpec(memory_space=pl.ANY)
    vmem = pl.BlockSpec(memory_space=pltpu.VMEM)
    return pl.pallas_call(
        functools.partial(step_kernel, (nband, ncomp, nsub)),
        out_shape=jax.ShapeDtypeStruct(orbitals.shape, f32),
        in_specs=[anywhere, vmem, anywhere, vmem, vmem],
        out_specs=anywhere,
        scratch_shapes=[
            pltpu.VMEM((norb, own), f32),
            pltpu.VMEM((norb + nproj, own), bf16),
            pltpu.VMEM((norb + nproj, own), bf16),
            pltpu.VMEM((full, TILE), f32),
            pltpu.VMEM((full, TILE), f32),
            pltpu.VMEM((norb, norb + nproj), bf16),
            pltpu.VMEM((norb, norb + nproj), bf16),
            pltpu.VMEM((norb, norb), bf16),
            pltpu.VMEM((norb, norb), bf16),
            pltpu.VMEM((norb, own), f32),
            pltpu.VMEM((nsub - 1, half, TILE), f32),
            pltpu.VMEM((ncomp - 1, nband, quarter // nband, TILE), f32),
            pltpu.VMEM((nband - 1, quarter // nband, TILE), f32),
            dma,
            dma((chunks, nband - 1)), dma((chunks, nband - 1)),
            dma((chunks, nband - 1)), dma((chunks, nband - 1)),
            dma((chunks,)),
            dma((2, nsub - 1)), dma((2, nsub - 1)),
            dma((2, ncomp - 1, nband)), dma((2, ncomp - 1, nband)),
            dma((2, nband - 1)), dma((2, nband - 1)),
            pltpu.VMEM((nproj, proj_len), f32), dma,
            *more,
        ],
        compiler_params=pltpu.CompilerParams(
            collective_id=0, has_side_effects=True, vmem_limit_bytes=48 * 1024 * 1024),
    )(orbitals, potential.reshape(1, row_width), proj, blocks, energy)


def solution(mesh):
    in_specs = (
        P(("groups", "band"), ("comp", "sub")),
        P(("groups", "comp", "sub")),
        P("groups", None, None),
        P("groups", None),
        P("groups", None),
    )
    out_specs = P(("groups", "band"), ("comp", "sub"))
    return jax.shard_map(
        on_device, mesh=mesh, in_specs=in_specs, out_specs=out_specs, check_vma=False
    )
```
